128 devices in a mesh: group: 64 (over z, y, x), blk: 2 (over core).
Axes of the slice: x: 4, y: 4, z: 4, core: 2. Of those that a mesh axis runs over, the one named last changes fastest.
Arguments:
- embeddings: bfloat16 [262144, 1024], P(('group', 'blk')), may hold values from -6 to 6
- cluster_ids: int32 [262144, 1], P(('group', 'blk')), may hold values from 0 to 255; in each aligned block of 2048 rows (0 to 2047, 2048 to 4095, ...) at most 16 rows name the same one
Outputs:
- nearest: float32 [262144], P(('group', 'blk'))
The draws below stay inside these ranges and needn't reach their ends.
Inputs may be any that keep to these rules, and one draw needn't show every extreme that they name: `cluster_ids`: among the rows of one device no cluster is named more than 16 times, a bound that some block reaches.
All inputs are finite; a program needn't handle non-finite values.
Results may differ from the reference program's by a relative error of at most 0.0014.
Values may be sent and summed in bfloat16 or wider, within the bound.
No kernel may reach another device: no remote copies, remote signals or barrier semaphores. Data moves between devices by JAX's collectives and lax.ppermute only.
A program may use at most 128 MiB of HBM per device.

```python
import math
import jax
import jax.numpy as jnp
import numpy as np
from jax import lax

D = 1024
ROWS_DEV = 2048
CLUSTERS = 256
MOST = 16
ROWS = 262144
N_GROUP = 64
N_BLK = 2


def shard_levels(rng, dims, split, low, largest):
    def one(axis_at, blocks):
        heights = jax.random.uniform(jax.random.fold_in(jax.random.fold_in(rng, 6), axis_at), (blocks,), jnp.float32, low / len(split), largest / len(split))
        return jnp.repeat(jnp.exp(heights), dims[axis_at] // blocks).reshape((-1,) + (1,) * (len(dims) - axis_at - 1))

    factor_of = one(*split[0])
    for cut in split[1:]:
        factor_of = factor_of * one(*cut)
    return factor_of


def deal_out(rng, own, number, rows, number_of, top, most, slope):
    order = jax.random.permutation(rng, number_of)
    packed, usual = shares(number_of, rows * top, most, slope, True), shares(number_of, rows * top, most, slope, False)
    places = jnp.arange(number_of)

    def named(tallies, offset_by):
        used = int((tallies > 0).sum())
        fixed = max(1, used // 4)
        shifted = fixed + (places - fixed + offset_by * (used - fixed)) % max(1, number_of - fixed)
        return jnp.zeros((number_of,), jnp.int32).at[order[jnp.where(places < fixed, places, shifted)]].set(jnp.asarray(tallies, jnp.int32))

    tallies = jnp.where(number % 4 == 0, named(packed, number // 4), named(usual, number - number // 4 - 1))
    mixed = jax.random.permutation(jax.random.fold_in(own, 3), number_of)
    donor, sink = mixed[0:number_of // 2 * 2:2], mixed[1:number_of // 2 * 2:2]
    room = jnp.minimum(tallies[donor] - 1, most - tallies[sink]) // 2
    room = jnp.where((donor == order[0]) | (sink == order[0]) | (tallies[sink] == 0), 0, jnp.maximum(room, 0))
    shifted = jax.random.randint(jax.random.fold_in(own, 4), (number_of // 2,), 0, 1 << 20) % (room + 1)
    tallies = tallies.at[donor].add(-shifted).at[sink].add(shifted)
    items = jnp.searchsorted(jnp.cumsum(tallies), jnp.arange(rows * top), side="right").astype(jnp.int32)
    listing = items.reshape(top, rows).T
    listing = listing[jax.random.permutation(jax.random.fold_in(own, 1), rows)]
    offset_by = jax.random.randint(jax.random.fold_in(own, 2), (rows, 1), 0, top)
    return jnp.take_along_axis(listing, (jnp.arange(top)[None, :] + offset_by) % top, axis=1)


def shares(number_of, total, most, skew, full):
    portions = [(1 << 20) // math.isqrt(grade ** skew) + 1 for grade in range(1, number_of + 1)]
    largest = most if full else min(most, max(-(-total // number_of), total * portions[0] // sum(portions)))
    least = 1 if total - largest >= number_of - 1 else 0
    counts, rest = [largest] + [least] * (number_of - 1), total - largest - least * (number_of - 1)
    while rest > 0:
        free = [i for i in range(1, number_of) if counts[i] < largest] or [i for i in range(1, number_of) if counts[i] < most]
        whole, left = sum([portions[i] for i in free]), rest
        for i in free:
            extra = min(most - counts[i], max(1, left * portions[i] // whole), rest)
            counts[i] = counts[i] + extra
            rest = rest - extra
    return np.array(counts)


def normal_values(own_key, dims, deviation, bound, shards=(), kind=jnp.bfloat16):
    level = shard_levels(own_key, dims, shards, -0.22, 0.18) if shards else 1.0
    entries = jax.random.normal(own_key, dims, jnp.float32) * deviation * level
    return jnp.minimum(jnp.maximum(entries, -bound), bound).astype(kind)


def setup_inputs(seed: int = 0) -> dict:
    splits = jax.random.split(jax.random.key(seed), 3)
    embeddings = normal_values(splits[0], (ROWS, D), 1.0, 6.0, ((0, 128),))
    cluster_ids_keys = jax.random.split(jax.random.fold_in(splits[1], 1), ROWS // ROWS_DEV)
    cluster_ids_turns = jax.random.permutation(jax.random.fold_in(splits[1], 3), ROWS // ROWS_DEV)
    cluster_ids = jax.vmap(lambda own, number: deal_out(jax.random.fold_in(splits[1], 2), own, number, ROWS_DEV, CLUSTERS, 1, MOST, 2))(cluster_ids_keys, cluster_ids_turns).reshape((ROWS, 1))
    return {"embeddings": embeddings, "cluster_ids": cluster_ids}


def reference(embeddings, cluster_ids):
    wide = embeddings.astype(jnp.float32)
    unit = (wide * lax.rsqrt(lax.optimization_barrier(jnp.sum(wide * wide, axis=1, keepdims=True)) + 1e-06)).astype(jnp.bfloat16)
    labels = cluster_ids[:, 0]
    capacity = N_GROUP * N_BLK * MOST

    def one_cluster(cluster):
        index = jnp.nonzero(labels == cluster, size=capacity, fill_value=ROWS)[0].astype(jnp.int32)
        inside = index < ROWS
        members = jnp.take(unit, index, axis=0, mode='fill', fill_value=0)
        similar = jnp.dot(members, members.T, preferred_element_type=jnp.float32)
        keep = inside[:, None] & inside[None, :] & (index[:, None] != index[None, :])
        return (index, lax.optimization_barrier(jnp.max(jnp.where(keep, similar, -1.0), axis=1)))
    index, best = lax.map(one_cluster, jnp.arange(CLUSTERS, dtype=jnp.int32))
    nearest = jnp.full((ROWS,), -1.0, jnp.float32)
    return nearest.at[index.reshape(-1)].set(best.reshape(-1), mode='drop')
```

```python
import jax
import jax.numpy as jnp
from jax import lax
from jax.experimental import pallas as pl
from jax.experimental.pallas import tpu as pltpu
from jax.sharding import PartitionSpec as P

CLUSTERS = 256
MOST = 16
PAD = 2.0
LANES = 128


def prep_kernel(x_hbm, label_ref, out_hbm, target_ref, xbuf, at_ref, rows, slots, obuf, where, in_sem, out_sem, where_sem):
    n, width = x_hbm.shape
    chunks = width // LANES
    total = out_hbm.shape[0]
    clusters = total // MOST
    parts = in_sem.shape[0]
    step = n // parts
    loads = [
        pltpu.make_async_copy(x_hbm.at[pl.ds(p * step, step)], xbuf.at[pl.ds(p * step, step)], in_sem.at[p])
        for p in range(parts)
    ]
    for load in loads:
        load.start()

    span = 256
    before = (
        lax.broadcasted_iota(jnp.int32, (span, span), 0) < lax.broadcasted_iota(jnp.int32, (span, span), 1)
    ).astype(jnp.bfloat16)
    carry = jnp.zeros((clusters, 1), jnp.float32)
    cluster = lax.broadcasted_iota(jnp.int32, (clusters, span), 0)
    for b in range(n // span):
        label = label_ref[:, b * span : (b + 1) * span]
        hit = cluster == label
        hot = jnp.where(hit, 1.0, 0.0)
        count = jnp.dot(hot.astype(jnp.bfloat16), before, preferred_element_type=jnp.float32) + carry
        rank = jnp.sum(jnp.where(hit, count, 0.0), axis=0, keepdims=True)
        carry = carry + jnp.sum(hot, axis=1, keepdims=True)
        target = label * MOST + rank.astype(jnp.int32)
        target_ref[:, b * span : (b + 1) * span] = target
        at_ref[:, b * span : (b + 1) * span] = (target // 8) * (8 * chunks) + target % 8
    place = pltpu.make_async_copy(at_ref, where, where_sem)
    place.start()

    def fill(i, _):
        base = pl.multiple_of(i * 64 * chunks, 64 * chunks)
        slots[pl.ds(base, 64 * chunks), :] = jnp.full((64 * chunks, LANES), PAD, jnp.float32)
        return 0

    lax.fori_loop(0, total // 64, fill, 0)

    for p in range(parts):
        loads[p].wait()

        def unit(i, _):
            r = pl.multiple_of(p * step + i * 16, 16)
            wide = xbuf[pl.ds(r, 16), :].astype(jnp.float32)
            scaled = wide * lax.rsqrt(jnp.sum(wide * wide, axis=1, keepdims=True) + 1e-06)
            base = pl.multiple_of(r * chunks, 16 * chunks)
            for h in range(2):
                for c in range(chunks):
                    rows[pl.ds(base + (h * chunks + c) * 8, 8), :] = scaled[h * 8 : h * 8 + 8, c * LANES : (c + 1) * LANES]
            return 0

        lax.fori_loop(0, step // 16, unit, 0, unroll=8)
    place.wait()

    def move(i, _):
        got = [rows[pl.ds(i * 16 * chunks + (u // 8) * 8 * chunks + u % 8, chunks, stride=8), :] for u in range(16)]
        for u in range(16):
            slots[pl.ds(where[0, i * 16 + u], chunks, stride=8), :] = got[u]
        return 0

    lax.fori_loop(0, n // 16, move, 0, unroll=8)

    oparts = out_sem.shape[0]
    ostep = total // oparts
    stores = []
    for p in range(oparts):

        def pack(i, _):
            r = pl.multiple_of(p * ostep + i * 16, 16)
            base = pl.multiple_of(r * chunks, 16 * chunks)
            lo = [slots[pl.ds(base + c * 8, 8), :] for c in range(chunks)]
            hi = [slots[pl.ds(base + (chunks + c) * 8, 8), :] for c in range(chunks)]
            both = [jnp.concatenate([a, b], axis=0).astype(jnp.bfloat16) for a, b in zip(lo, hi)]
            for c in range(chunks):
                obuf[pl.ds(r, 16), c * LANES : (c + 1) * LANES] = both[c]
            return 0

        lax.fori_loop(0, ostep // 16, pack, 0, unroll=8)
        store = pltpu.make_async_copy(obuf.at[pl.ds(p * ostep, ostep)], out_hbm.at[pl.ds(p * ostep, ostep)], out_sem.at[p])
        store.start()
        stores.append(store)
    for store in stores:
        store.wait()


def prep(x, labels, clusters):
    n, width = x.shape
    total = clusters * MOST
    chunks = width // LANES
    return pl.pallas_call(
        prep_kernel,
        out_shape=(
            jax.ShapeDtypeStruct((total, width), jnp.bfloat16),
            jax.ShapeDtypeStruct((1, n), jnp.int32),
        ),
        in_specs=[pl.BlockSpec(memory_space=pl.ANY), pl.BlockSpec(memory_space=pltpu.VMEM)],
        out_specs=(pl.BlockSpec(memory_space=pl.ANY), pl.BlockSpec(memory_space=pltpu.VMEM)),
        scratch_shapes=[
            pltpu.VMEM((n, width), jnp.bfloat16),
            pltpu.VMEM((1, n), jnp.int32),
            pltpu.VMEM((n * chunks, LANES), jnp.float32),
            pltpu.VMEM((total * chunks, LANES), jnp.float32),
            pltpu.VMEM((total, width), jnp.bfloat16),
            pltpu.SMEM((1, n), jnp.int32),
            pltpu.SemaphoreType.DMA((8,)),
            pltpu.SemaphoreType.DMA((8,)),
            pltpu.SemaphoreType.DMA(()),
        ],
        compiler_params=pltpu.CompilerParams(vmem_limit_bytes=52 * 1024 * 1024),
        name="prep",
    )(x, labels)


def near_kernel(x_hbm, out_ref, rows, bias, row_best, col_best, packed, sem):
    sources, pair, width = x_hbm.shape
    per = pair // MOST
    n = sources * MOST
    tile = 256
    blocks = n // tile
    src_tile = tile // MOST
    loads = [
        [
            pltpu.make_async_copy(
                x_hbm.at[pl.ds(b * src_tile, src_tile), pl.ds(k * MOST, MOST), :],
                rows.at[k, pl.ds(b * src_tile, src_tile)],
                sem.at[k, b],
            )
            for b in range(blocks)
        ]
        for k in range(per)
    ]
    for k in range(per):
        for b in range(blocks):
            loads[k][b].start()
    first = (lax.broadcasted_iota(jnp.int32, (8, LANES), 1) == 0).astype(jnp.bfloat16)
    contract = (((1,), (1,)), ((), ()))
    diagonal = lax.broadcasted_iota(jnp.int32, (tile, tile), 0) == lax.broadcasted_iota(jnp.int32, (tile, tile), 1)
    for k in range(per):
        for b in range(blocks):
            loads[k][b].wait()
            mine = rows[k, b * src_tile : (b + 1) * src_tile].reshape(tile, width)
            mark = lax.dot_general(first, mine[:, :LANES], contract, preferred_element_type=jnp.float32)[0:1]
            col_bias = jnp.where(mark > 1.5, -1000.0, 0.0)
            row_mark = mine[:, 0:1].astype(jnp.float32)
            bias[b * tile : (b + 1) * tile, :] = jnp.broadcast_to(jnp.where(row_mark > 1.5, -1000.0, 0.0), (tile, LANES))
            best = None
            for a in range(b + 1):
                theirs = rows[k, a * src_tile : (a + 1) * src_tile].reshape(tile, width)
                similar = lax.dot_general(theirs, mine, contract, preferred_element_type=jnp.float32)
                if a == b:
                    similar = jnp.where(diagonal, -1000.0, similar)
                across = similar + col_bias
                across = jnp.maximum(across[:, :LANES], across[:, LANES:])
                down = similar + bias[a * tile : (a + 1) * tile, 0:1]
                down = jnp.max(down, axis=0, keepdims=True)
                if a == b:
                    row_best[a * tile : (a + 1) * tile, :] = across
                else:
                    row_best[a * tile : (a + 1) * tile, :] = jnp.maximum(row_best[a * tile : (a + 1) * tile, :], across)
                    best = down if best is None else jnp.maximum(best, down)
            if best is None:
                best = jnp.full((1, tile), -1.0, jnp.float32)
            col_best[:, b * tile : (b + 1) * tile] = jnp.maximum(best, -1.0)
        for b in range(blocks):
            across = jnp.max(row_best[b * tile : (b + 1) * tile, :].T, axis=0, keepdims=True)
            best = jnp.maximum(across, col_best[:, b * tile : (b + 1) * tile])
            for h in range(tile // LANES):
                q = b * (tile // LANES) + h
                packed[q : q + 1, :] = best[:, h * LANES : (h + 1) * LANES]
        group = LANES // MOST
        for g in range(group):
            out_ref[:, g, k * MOST : (k + 1) * MOST] = packed[:, g * MOST : (g + 1) * MOST]


def near(x, per):
    sources, pair, width = x.shape
    n = sources * MOST
    group = LANES // MOST
    return pl.pallas_call(
        near_kernel,
        out_shape=jax.ShapeDtypeStruct((sources // group, group, pair), jnp.float32),
        in_specs=[pl.BlockSpec(memory_space=pl.ANY)],
        out_specs=pl.BlockSpec(memory_space=pltpu.VMEM),
        scratch_shapes=[
            pltpu.VMEM((per, sources, MOST, width), jnp.bfloat16),
            pltpu.VMEM((n, LANES), jnp.float32),
            pltpu.VMEM((n, LANES), jnp.float32),
            pltpu.VMEM((1, n), jnp.float32),
            pltpu.VMEM((n // LANES, LANES), jnp.float32),
            pltpu.SemaphoreType.DMA((per, n // 256)),
        ],
        compiler_params=pltpu.CompilerParams(vmem_limit_bytes=48 * 1024 * 1024),
        name="near",
    )(x)


def pick_kernel(x_ref, target_ref, out_ref):
    owners, pair = x_ref.shape
    n = target_ref.shape[1]
    table = x_ref[...].T
    hi = table.astype(jnp.bfloat16)
    rest = table - hi.astype(jnp.float32)
    mid = rest.astype(jnp.bfloat16)
    low = (rest - mid.astype(jnp.float32)).astype(jnp.bfloat16)
    split = jnp.concatenate([hi, mid, low], axis=0)
    span = 512
    owner = lax.broadcasted_iota(jnp.int32, (owners, span), 0)
    slot = lax.broadcasted_iota(jnp.int32, (pair, span), 0)
    for b in range(n // span):
        target = target_ref[:, b * span : (b + 1) * span]
        hot = jnp.where(owner == target // pair, 1.0, 0.0).astype(jnp.bfloat16)
        got = jnp.dot(split, hot, preferred_element_type=jnp.float32)
        value = (got[:pair] + got[pair : 2 * pair]) + got[2 * pair :]
        out_ref[:, b * span : (b + 1) * span] = jnp.sum(
            jnp.where(slot == target % pair, value, 0.0), axis=0, keepdims=True
        )


def pick(x, target):
    return pl.pallas_call(
        pick_kernel,
        out_shape=jax.ShapeDtypeStruct(target.shape, jnp.float32),
        name="pick",
    )(x, target)


def per_device(embeddings, cluster_ids):
    n = embeddings.shape[0]
    axes = ("group", "blk")
    devices = lax.axis_size("group") * lax.axis_size("blk")
    per = CLUSTERS // devices
    outgoing, target = prep(embeddings, cluster_ids.reshape(1, n), CLUSTERS)
    outgoing = outgoing.reshape(devices, per * MOST, -1)
    members = lax.all_to_all(outgoing, axes, split_axis=0, concat_axis=0, tiled=True)
    best = near(members, per).reshape(devices, per * MOST)
    results = lax.all_to_all(best, axes, split_axis=0, concat_axis=0, tiled=True)
    return pick(results, target).reshape(n)


def solution(mesh):
    placed = (P(("group", "blk"), None), P(("group", "blk"), None))
    return jax.shard_map(
        per_device, mesh=mesh, in_specs=placed, out_specs=P(("group", "blk")), check_vma=False
    )
```

```python
import jax
import jax.numpy as jnp
from jax import lax
from jax.experimental import pallas as pl
from jax.experimental.pallas import tpu as pltpu
from jax.sharding import PartitionSpec as P

CLUSTERS = 256
MOST = 16
LANES = 128
PAD = 2.0
FAR = -1000.0
PITCH = 9


def prep_kernel(
    x_hbm, label_hbm, out_hbm, target_ref, xbuf, label, at, rows, slots, obuf, where, in_sem, out_sem, small_sem
):
    n, width = x_hbm.shape
    chunks = width // LANES
    total = out_hbm.shape[0]
    clusters = total // MOST
    pitch = PITCH * chunks
    parts = in_sem.shape[0]
    step = n // parts
    fetch = pltpu.make_async_copy(label_hbm, label, small_sem.at[0])
    fetch.start()
    loads = [
        pltpu.make_async_copy(x_hbm.at[pl.ds(p * step, step)], xbuf.at[pl.ds(p * step, step)], in_sem.at[p])
        for p in range(parts)
    ]
    for load in loads:
        load.start()

    def fill(i, _):
        base = pl.multiple_of(i * 8 * pitch, 8 * pitch)
        slots[pl.ds(base, 8 * pitch), :] = jnp.full((8 * pitch, LANES), PAD, jnp.float32)
        return 0

    lax.fori_loop(0, total // 64, fill, 0)
    fetch.wait()
    span = 256
    before = (
        lax.broadcasted_iota(jnp.int32, (span, span), 0) < lax.broadcasted_iota(jnp.int32, (span, span), 1)
    ).astype(jnp.bfloat16)
    carry = jnp.zeros((clusters, 1), jnp.float32)
    cluster = lax.broadcasted_iota(jnp.int32, (clusters, span), 0)
    for b in range(n // span):
        name = label[:, b * span : (b + 1) * span]
        hit = cluster == name
        hot = jnp.where(hit, 1.0, 0.0)
        count = jnp.dot(hot.astype(jnp.bfloat16), before, preferred_element_type=jnp.float32) + carry
        rank = jnp.sum(jnp.where(hit, count, 0.0), axis=0, keepdims=True)
        carry = carry + jnp.sum(hot, axis=1, keepdims=True)
        target = name * MOST + rank.astype(jnp.int32)
        target_ref[:, b * span : (b + 1) * span] = target
        at[:, b * span : (b + 1) * span] = (target >> 3) * pitch + (target & 7)
    place = pltpu.make_async_copy(at, where, small_sem.at[1])
    place.start()

    for p in range(parts):
        loads[p].wait()

        def unit(i, _):
            r = pl.multiple_of(p * step + i * 16, 16)
            wide = xbuf[pl.ds(r, 16), :].astype(jnp.float32)
            scaled = wide * lax.rsqrt(jnp.sum(wide * wide, axis=1, keepdims=True) + 1e-06)
            base = (r >> 3) * pitch
            for h in range(2):
                for c in range(chunks):
                    rows[pl.ds(base + h * pitch + c * PITCH, 8), :] = scaled[
                        h * 8 : h * 8 + 8, c * LANES : (c + 1) * LANES
                    ]
            return 0

        lax.fori_loop(0, step // 16, unit, 0, unroll=step // 16)
    place.wait()
    batch = 64

    def move(i, _):
        got = [rows[pl.ds((i * (batch // 8) + u // 8) * pitch + u % 8, chunks, stride=PITCH), :] for u in range(batch)]
        for u in range(batch):
            slots[pl.ds(where[0, i * batch + u], chunks, stride=PITCH), :] = got[u]
        return 0

    lax.fori_loop(0, n // batch, move, 0, unroll=2)

    out_parts = out_sem.shape[0]
    out_step = total // out_parts
    stores = []
    for p in range(out_parts):

        def pack(i, _):
            r = pl.multiple_of(p * out_step + i * 16, 16)
            base = (r >> 3) * pitch
            low = [slots[pl.ds(base + c * PITCH, 8), :] for c in range(chunks)]
            high = [slots[pl.ds(base + pitch + c * PITCH, 8), :] for c in range(chunks)]
            both = [jnp.concatenate([a, b], axis=0).astype(jnp.bfloat16) for a, b in zip(low, high)]
            for c in range(chunks):
                obuf[pl.ds(r, 16), c * LANES : (c + 1) * LANES] = both[c]
            return 0

        lax.fori_loop(0, out_step // 16, pack, 0, unroll=8)
        store = pltpu.make_async_copy(
            obuf.at[pl.ds(p * out_step, out_step)], out_hbm.at[pl.ds(p * out_step, out_step)], out_sem.at[p]
        )
        store.start()
        stores.append(store)
    for store in stores:
        store.wait()


def prep(x, labels, clusters):
    n, width = x.shape
    total = clusters * MOST
    chunks = width // LANES
    return pl.pallas_call(
        prep_kernel,
        out_shape=(
            jax.ShapeDtypeStruct((total, width), jnp.bfloat16),
            jax.ShapeDtypeStruct((1, n), jnp.int32),
        ),
        in_specs=[pl.BlockSpec(memory_space=pl.ANY), pl.BlockSpec(memory_space=pltpu.HBM)],
        out_specs=(pl.BlockSpec(memory_space=pl.ANY), pl.BlockSpec(memory_space=pltpu.VMEM)),
        scratch_shapes=[
            pltpu.VMEM((n, width), jnp.bfloat16),
            pltpu.VMEM((1, n), jnp.int32),
            pltpu.VMEM((1, n), jnp.int32),
            pltpu.VMEM((n * PITCH // 8 * chunks, LANES), jnp.float32),
            pltpu.VMEM((total * PITCH // 8 * chunks, LANES), jnp.float32),
            pltpu.VMEM((total, width), jnp.bfloat16),
            pltpu.SMEM((1, n), jnp.int32),
            pltpu.SemaphoreType.DMA((4,)),
            pltpu.SemaphoreType.DMA((8,)),
            pltpu.SemaphoreType.DMA((2,)),
        ],
        compiler_params=pltpu.CompilerParams(vmem_limit_bytes=60 * 1024 * 1024),
        name="prep",
    )(x, labels)


def near_plan(per, blocks):
    cuts = [0] + [c for c in (1, 2, 4) if c < blocks] + [blocks]
    first = [(0, low, high) for low, high in zip(cuts[:-1], cuts[1:])]
    return first + [(k, 0, blocks) for k in range(1, per)]


def near_kernel(x_hbm, out_ref, rows, bias, row_best, col_best, packed, sem):
    sources, pair, width = x_hbm.shape
    per = pair // MOST
    tile = 256
    from_each = tile // MOST
    blocks = sources // from_each
    plan = near_plan(per, blocks)
    loads = [
        pltpu.make_async_copy(
            x_hbm.at[pl.ds(low * from_each, (high - low) * from_each), pl.ds(k * MOST, MOST), :],
            rows.at[k, pl.ds(low * from_each, (high - low) * from_each)],
            sem.at[i],
        )
        for i, (k, low, high) in enumerate(plan)
    ]
    for load in loads:
        load.start()
    contract = (((1,), (1,)), ((), ()))
    first = (lax.broadcasted_iota(jnp.int32, (8, LANES), 1) == 0).astype(jnp.bfloat16)
    diagonal = lax.broadcasted_iota(jnp.int32, (tile, tile), 0) == lax.broadcasted_iota(jnp.int32, (tile, tile), 1)

    def finish(k):
        for b in range(blocks):
            across = jnp.max(row_best[k, b * tile : (b + 1) * tile, :].T, axis=0, keepdims=True)
            best = jnp.maximum(across, col_best[k : k + 1, b * tile : (b + 1) * tile])
            for h in range(tile // LANES):
                q = b * (tile // LANES) + h
                packed[k, q : q + 1, :] = best[:, h * LANES : (h + 1) * LANES]
        for g in range(LANES // MOST):
            out_ref[:, g, k * MOST : (k + 1) * MOST] = packed[k, :, g * MOST : (g + 1) * MOST]

    for i, (k, low, high) in enumerate(plan):
        loads[i].wait()
        if k > 0 and low == 0:
            finish(k - 1)
        for b in range(low, high):
            mine = rows[k, b * from_each : (b + 1) * from_each].reshape(tile, width)
            row_mark = mine[:, 0:1].astype(jnp.float32)
            bias[k, b * tile : (b + 1) * tile, :] = jnp.broadcast_to(jnp.where(row_mark > 1.5, FAR, 0.0), (tile, LANES))
            col_mark = lax.dot_general(first, mine[:, :LANES], contract, preferred_element_type=jnp.float32)[0:1]
            col_bias = jnp.where(col_mark > 1.5, FAR, 0.0)
            best = jnp.full((8, tile), -1.0, jnp.float32)
            for a in [b] + list(range(b)):
                theirs = rows[k, a * from_each : (a + 1) * from_each].reshape(tile, width)
                similar = lax.dot_general(theirs, mine, contract, preferred_element_type=jnp.float32)
                if a == b:
                    similar = jnp.where(diagonal, FAR, similar)
                across = similar + col_bias
                across = jnp.maximum(across[:, :LANES], across[:, LANES:])
                if a == b:
                    row_best[k, a * tile : (a + 1) * tile, :] = across
                else:
                    row_best[k, a * tile : (a + 1) * tile, :] = jnp.maximum(
                        row_best[k, a * tile : (a + 1) * tile, :], across
                    )
                    down = similar + bias[k, a * tile : (a + 1) * tile, 0:1]
                    best = jnp.maximum(best, jnp.max(down.reshape(tile // 8, 8, tile), axis=0))
            col_best[k : k + 1, b * tile : (b + 1) * tile] = jnp.max(best, axis=0, keepdims=True)
    finish(per - 1)


def near(x, per):
    sources, pair, width = x.shape
    n = sources * MOST
    group = LANES // MOST
    return pl.pallas_call(
        near_kernel,
        out_shape=jax.ShapeDtypeStruct((sources // group, group, pair), jnp.float32),
        in_specs=[pl.BlockSpec(memory_space=pl.ANY)],
        out_specs=pl.BlockSpec(memory_space=pltpu.VMEM),
        scratch_shapes=[
            pltpu.VMEM((per, sources, MOST, width), jnp.bfloat16),
            pltpu.VMEM((per, n, LANES), jnp.float32),
            pltpu.VMEM((per, n, LANES), jnp.float32),
            pltpu.VMEM((per, n), jnp.float32),
            pltpu.VMEM((per, n // LANES, LANES), jnp.float32),
            pltpu.SemaphoreType.DMA((len(near_plan(per, n // 256)),)),
        ],
        compiler_params=pltpu.CompilerParams(vmem_limit_bytes=48 * 1024 * 1024),
        name="near",
    )(x)


def pick_kernel(x_ref, target_ref, out_ref):
    owners, pair = x_ref.shape
    n = target_ref.shape[1]
    table = x_ref[...].T
    hi = table.astype(jnp.bfloat16)
    rest = table - hi.astype(jnp.float32)
    mid = rest.astype(jnp.bfloat16)
    low = (rest - mid.astype(jnp.float32)).astype(jnp.bfloat16)
    split = jnp.concatenate([hi, mid, low], axis=0)
    span = 512
    owner = lax.broadcasted_iota(jnp.int32, (owners, span), 0)
    slot = lax.broadcasted_iota(jnp.int32, (pair, span), 0)
    for b in range(n // span):
        target = target_ref[:, b * span : (b + 1) * span]
        hot = jnp.where(owner == target // pair, 1.0, 0.0).astype(jnp.bfloat16)
        got = jnp.dot(split, hot, preferred_element_type=jnp.float32)
        value = (got[:pair] + got[pair : 2 * pair]) + got[2 * pair :]
        out_ref[:, b * span : (b + 1) * span] = jnp.sum(
            jnp.where(slot == target % pair, value, 0.0), axis=0, keepdims=True
        )


def pick(x, target):
    return pl.pallas_call(
        pick_kernel,
        out_shape=jax.ShapeDtypeStruct(target.shape, jnp.float32),
        name="pick",
    )(x, target)


def per_device(embeddings, cluster_ids):
    n = embeddings.shape[0]
    axes = ("group", "blk")
    devices = lax.axis_size("group") * lax.axis_size("blk")
    per = CLUSTERS // devices
    outgoing, target = prep(embeddings, cluster_ids.reshape(1, n), CLUSTERS)
    outgoing = outgoing.reshape(devices, per * MOST, -1)
    members = lax.all_to_all(outgoing, axes, split_axis=0, concat_axis=0, tiled=True)
    best = near(members, per).reshape(devices, per * MOST)
    results = lax.all_to_all(best, axes, split_axis=0, concat_axis=0, tiled=True)
    return pick(results, target).reshape(n)


def solution(mesh):
    placed = (P(("group", "blk"), None), P(("group", "blk"), None))
    return jax.shard_map(
        per_device, mesh=mesh, in_specs=placed, out_specs=P(("group", "blk")), check_vma=False
    )
```

```python
import jax
import jax.numpy as jnp
from jax import lax
from jax.experimental import pallas as pl
from jax.experimental.pallas import tpu as pltpu
from jax.sharding import PartitionSpec as P

CLUSTERS = 256
MOST = 16
LANES = 128
PAD = 2.0
FAR = -1000.0
PITCH = 9


def prep_kernel(
    x_hbm, label_hbm, out_hbm, target_ref, xbuf, label, at, rows, slots, obuf, where, in_sem, out_sem, small_sem
):
    n, width = x_hbm.shape
    chunks = width // LANES
    total = out_hbm.shape[0]
    clusters = total // MOST
    pitch = PITCH * chunks
    parts = in_sem.shape[0]
    step = n // parts
    fetch = pltpu.make_async_copy(label_hbm, label, small_sem.at[0])
    fetch.start()
    loads = [
        pltpu.make_async_copy(x_hbm.at[pl.ds(p * step, step)], xbuf.at[pl.ds(p * step, step)], in_sem.at[p])
        for p in range(parts)
    ]
    for load in loads:
        load.start()

    def fill(i, _):
        base = pl.multiple_of(i * 8 * pitch, 8 * pitch)
        slots[pl.ds(base, 8 * pitch), :] = jnp.full((8 * pitch, LANES), PAD, jnp.float32)
        return 0

    lax.fori_loop(0, total // 64, fill, 0)
    fetch.wait()
    span = 256
    before = (
        lax.broadcasted_iota(jnp.int32, (span, span), 0) < lax.broadcasted_iota(jnp.int32, (span, span), 1)
    ).astype(jnp.bfloat16)
    carry = jnp.zeros((clusters, 1), jnp.float32)
    cluster = lax.broadcasted_iota(jnp.int32, (clusters, span), 0)
    for b in range(n // span):
        name = label[:, b * span : (b + 1) * span]
        hit = cluster == name
        hot = jnp.where(hit, 1.0, 0.0)
        count = jnp.dot(hot.astype(jnp.bfloat16), before, preferred_element_type=jnp.float32) + carry
        rank = jnp.sum(jnp.where(hit, count, 0.0), axis=0, keepdims=True)
        carry = carry + jnp.sum(hot, axis=1, keepdims=True)
        target = name * MOST + rank.astype(jnp.int32)
        target_ref[:, b * span : (b + 1) * span] = target
        at[:, b * span : (b + 1) * span] = (target >> 3) * pitch + (target & 7)
    place = pltpu.make_async_copy(at, where, small_sem.at[1])
    place.start()

    for p in range(parts):
        loads[p].wait()

        for r in range(p * step, (p + 1) * step, 16):
            wide = xbuf[r : r + 16, :].astype(jnp.float32)
            scaled = wide * lax.rsqrt(jnp.sum(wide * wide, axis=1, keepdims=True) + 1e-06)
            for h in range(2):
                for c in range(chunks):
                    low = (r // 8 + h) * pitch + c * PITCH
                    rows[low : low + 8, :] = scaled[h * 8 : h * 8 + 8, c * LANES : (c + 1) * LANES]
    place.wait()
    batch = 16

    def move(i, _):
        got = [rows[pl.ds((i * (batch // 8) + u // 8) * pitch + u % 8, chunks, stride=PITCH), :] for u in range(batch)]
        for u in range(batch):
            slots[pl.ds(where[0, i * batch + u], chunks, stride=PITCH), :] = got[u]
        return 0

    lax.fori_loop(0, n // batch, move, 0, unroll=n // batch)

    out_parts = out_sem.shape[0]
    out_step = total // out_parts
    stores = []
    for p in range(out_parts):

        def pack(i, _):
            r = pl.multiple_of(p * out_step + i * 16, 16)
            base = (r >> 3) * pitch
            low = [slots[pl.ds(base + c * PITCH, 8), :] for c in range(chunks)]
            high = [slots[pl.ds(base + pitch + c * PITCH, 8), :] for c in range(chunks)]
            both = [jnp.concatenate([a, b], axis=0).astype(jnp.bfloat16) for a, b in zip(low, high)]
            for c in range(chunks):
                obuf[pl.ds(r, 16), c * LANES : (c + 1) * LANES] = both[c]
            return 0

        lax.fori_loop(0, out_step // 16, pack, 0, unroll=out_step // 16)
        store = pltpu.make_async_copy(
            obuf.at[pl.ds(p * out_step, out_step)], out_hbm.at[pl.ds(p * out_step, out_step)], out_sem.at[p]
        )
        store.start()
        stores.append(store)
    for store in stores:
        store.wait()


def prep(x, labels, clusters):
    n, width = x.shape
    total = clusters * MOST
    chunks = width // LANES
    return pl.pallas_call(
        prep_kernel,
        out_shape=(
            jax.ShapeDtypeStruct((total, width), jnp.bfloat16),
            jax.ShapeDtypeStruct((1, n), jnp.int32),
        ),
        in_specs=[pl.BlockSpec(memory_space=pl.ANY), pl.BlockSpec(memory_space=pltpu.HBM)],
        out_specs=(pl.BlockSpec(memory_space=pl.ANY), pl.BlockSpec(memory_space=pltpu.VMEM)),
        scratch_shapes=[
            pltpu.VMEM((n, width), jnp.bfloat16),
            pltpu.VMEM((1, n), jnp.int32),
            pltpu.VMEM((1, n), jnp.int32),
            pltpu.VMEM((n * PITCH // 8 * chunks, LANES), jnp.float32),
            pltpu.VMEM((total * PITCH // 8 * chunks, LANES), jnp.float32),
            pltpu.VMEM((total, width), jnp.bfloat16),
            pltpu.SMEM((1, n), jnp.int32),
            pltpu.SemaphoreType.DMA((4,)),
            pltpu.SemaphoreType.DMA((8,)),
            pltpu.SemaphoreType.DMA((2,)),
        ],
        compiler_params=pltpu.CompilerParams(vmem_limit_bytes=60 * 1024 * 1024),
        name="prep",
    )(x, labels)


def near_plan(per, blocks):
    cuts = [0] + [c for c in (1, 2, 4) if c < blocks] + [blocks]
    first = [(0, low, high) for low, high in zip(cuts[:-1], cuts[1:])]
    return first + [(k, 0, blocks) for k in range(1, per)]


def near_kernel(x_hbm, out_ref, rows, bias, row_best, col_best, packed, sem):
    sources, pair, width = x_hbm.shape
    per = pair // MOST
    tile = 256
    from_each = tile // MOST
    blocks = sources // from_each
    plan = near_plan(per, blocks)
    loads = [
        pltpu.make_async_copy(
            x_hbm.at[pl.ds(low * from_each, (high - low) * from_each), pl.ds(k * MOST, MOST), :],
            rows.at[k, pl.ds(low * from_each, (high - low) * from_each)],
            sem.at[i],
        )
        for i, (k, low, high) in enumerate(plan)
    ]
    for load in loads:
        load.start()
    contract = (((1,), (1,)), ((), ()))
    first = (lax.broadcasted_iota(jnp.int32, (8, LANES), 1) == 0).astype(jnp.bfloat16)
    diagonal = lax.broadcasted_iota(jnp.int32, (tile, tile), 0) == lax.broadcasted_iota(jnp.int32, (tile, tile), 1)

    def finish(k):
        for b in range(blocks):
            across = jnp.max(row_best[k, b * tile : (b + 1) * tile, :].T, axis=0, keepdims=True)
            best = jnp.maximum(across, col_best[k : k + 1, b * tile : (b + 1) * tile])
            for h in range(tile // LANES):
                q = b * (tile // LANES) + h
                packed[k, q : q + 1, :] = best[:, h * LANES : (h + 1) * LANES]
        for g in range(LANES // MOST):
            out_ref[:, g, k * MOST : (k + 1) * MOST] = packed[k, :, g * MOST : (g + 1) * MOST]

    for i, (k, low, high) in enumerate(plan):
        loads[i].wait()
        if k > 0 and low == 0:
            finish(k - 1)
        for b in range(low, high):
            mine = rows[k, b * from_each : (b + 1) * from_each].reshape(tile, width)
            row_mark = mine[:, 0:1].astype(jnp.float32)
            bias[k, b * tile : (b + 1) * tile, :] = jnp.broadcast_to(jnp.where(row_mark > 1.5, FAR, 0.0), (tile, LANES))
            col_mark = lax.dot_general(first, mine[:, :LANES], contract, preferred_element_type=jnp.float32)[0:1]
            col_bias = jnp.where(col_mark > 1.5, FAR, 0.0)
            best = jnp.full((8, tile), -1.0, jnp.float32)
            for a in [b] + list(range(b)):
                theirs = rows[k, a * from_each : (a + 1) * from_each].reshape(tile, width)
                similar = lax.dot_general(theirs, mine, contract, preferred_element_type=jnp.float32)
                if a == b:
                    similar = jnp.where(diagonal, FAR, similar)
                across = similar + col_bias
                across = jnp.maximum(across[:, :LANES], across[:, LANES:])
                if a == b:
                    row_best[k, a * tile : (a + 1) * tile, :] = across
                else:
                    row_best[k, a * tile : (a + 1) * tile, :] = jnp.maximum(
                        row_best[k, a * tile : (a + 1) * tile, :], across
                    )
                    down = similar + bias[k, a * tile : (a + 1) * tile, 0:1]
                    best = jnp.maximum(best, jnp.max(down.reshape(tile // 8, 8, tile), axis=0))
            col_best[k : k + 1, b * tile : (b + 1) * tile] = jnp.max(best, axis=0, keepdims=True)
    finish(per - 1)


def near(x, per):
    sources, pair, width = x.shape
    n = sources * MOST
    group = LANES // MOST
    return pl.pallas_call(
        near_kernel,
        out_shape=jax.ShapeDtypeStruct((sources // group, group, pair), jnp.float32),
        in_specs=[pl.BlockSpec(memory_space=pl.ANY)],
        out_specs=pl.BlockSpec(memory_space=pltpu.VMEM),
        scratch_shapes=[
            pltpu.VMEM((per, sources, MOST, width), jnp.bfloat16),
            pltpu.VMEM((per, n, LANES), jnp.float32),
            pltpu.VMEM((per, n, LANES), jnp.float32),
            pltpu.VMEM((per, n), jnp.float32),
            pltpu.VMEM((per, n // LANES, LANES), jnp.float32),
            pltpu.SemaphoreType.DMA((len(near_plan(per, n // 256)),)),
        ],
        compiler_params=pltpu.CompilerParams(vmem_limit_bytes=48 * 1024 * 1024),
        name="near",
    )(x)


def pick_kernel(x_ref, target_ref, out_ref):
    owners, pair = x_ref.shape
    n = target_ref.shape[1]
    table = x_ref[...].T
    hi = table.astype(jnp.bfloat16)
    rest = table - hi.astype(jnp.float32)
    mid = rest.astype(jnp.bfloat16)
    low = (rest - mid.astype(jnp.float32)).astype(jnp.bfloat16)
    split = jnp.concatenate([hi, mid, low], axis=0)
    shift = pair.bit_length() - 1
    span = 1024
    owner = lax.broadcasted_iota(jnp.int32, (owners, span), 0)
    slot = lax.broadcasted_iota(jnp.int32, (pair, span), 0)
    for b in range(n // span):
        target = target_ref[:, b * span : (b + 1) * span]
        hot = jnp.where(owner == target >> shift, 1.0, 0.0).astype(jnp.bfloat16)
        got = jnp.dot(split, hot, preferred_element_type=jnp.float32)
        value = (got[:pair] + got[pair : 2 * pair]) + got[2 * pair :]
        out_ref[:, b * span : (b + 1) * span] = jnp.sum(
            jnp.where(slot == (target & (pair - 1)), value, 0.0), axis=0, keepdims=True
        )


def pick(x, target):
    return pl.pallas_call(
        pick_kernel,
        out_shape=jax.ShapeDtypeStruct(target.shape, jnp.float32),
        name="pick",
    )(x, target)


def per_device(embeddings, cluster_ids):
    n = embeddings.shape[0]
    axes = ("group", "blk")
    devices = lax.axis_size("group") * lax.axis_size("blk")
    per = CLUSTERS // devices
    outgoing, target = prep(embeddings, cluster_ids.reshape(1, n), CLUSTERS)
    outgoing = outgoing.reshape(devices, per * MOST, -1)
    members = lax.all_to_all(outgoing, axes, split_axis=0, concat_axis=0, tiled=True)
    best = near(members, per).reshape(devices, per * MOST)
    results = lax.all_to_all(best, axes, split_axis=0, concat_axis=0, tiled=True)
    return pick(results, target).reshape(n)


def solution(mesh):
    placed = (P(("group", "blk"), None), P(("group", "blk"), None))
    return jax.shard_map(
        per_device, mesh=mesh, in_specs=placed, out_specs=P(("group", "blk")), check_vma=False
    )
```

```python
import jax
import jax.numpy as jnp
from jax import lax
from jax.experimental import pallas as pl
from jax.experimental.pallas import tpu as pltpu
from jax.sharding import PartitionSpec as P

CLUSTERS = 256
MOST = 16
LANES = 128
PAD = 2.0
FAR = -1000.0
PITCH = 9


def prep_kernel(
    x_hbm, label_hbm, out_hbm, target_ref, xbuf, label, at, rows, slots, obuf, where, in_sem, out_sem, small_sem
):
    n, width = x_hbm.shape
    chunks = width // LANES
    total = out_hbm.shape[0]
    clusters = total // MOST
    pitch = PITCH * chunks
    parts = in_sem.shape[0]
    step = n // parts
    fetch = pltpu.make_async_copy(label_hbm, label, small_sem.at[0])
    fetch.start()
    loads = [
        pltpu.make_async_copy(x_hbm.at[pl.ds(p * step, step)], xbuf.at[pl.ds(p * step, step)], in_sem.at[p])
        for p in range(parts)
    ]
    for load in loads:
        load.start()

    def fill(i, _):
        base = pl.multiple_of(i * 8 * pitch, 8 * pitch)
        slots[pl.ds(base, 8 * pitch), :] = jnp.full((8 * pitch, LANES), PAD, jnp.float32)
        return 0

    lax.fori_loop(0, total // 64, fill, 0)
    fetch.wait()
    span = 256
    before = (
        lax.broadcasted_iota(jnp.int32, (span, span), 0) < lax.broadcasted_iota(jnp.int32, (span, span), 1)
    ).astype(jnp.bfloat16)
    carry = jnp.zeros((clusters, 1), jnp.float32)
    cluster = lax.broadcasted_iota(jnp.int32, (clusters, span), 0)
    for b in range(n // span):
        name = label[:, b * span : (b + 1) * span]
        hit = cluster == name
        hot = jnp.where(hit, 1.0, 0.0)
        count = jnp.dot(hot.astype(jnp.bfloat16), before, preferred_element_type=jnp.float32) + carry
        rank = jnp.sum(jnp.where(hit, count, 0.0), axis=0, keepdims=True)
        carry = carry + jnp.sum(hot, axis=1, keepdims=True)
        target = name * MOST + rank.astype(jnp.int32)
        target_ref[:, b * span : (b + 1) * span] = target
        at[:, b * span : (b + 1) * span] = (target >> 3) * pitch + (target & 7)
    place = pltpu.make_async_copy(at, where, small_sem.at[1])
    place.start()

    for p in range(parts):
        loads[p].wait()

        for r in range(p * step, (p + 1) * step, 16):
            wide = xbuf[r : r + 16, :].astype(jnp.float32)
            scaled = wide * lax.rsqrt(jnp.sum(wide * wide, axis=1, keepdims=True) + 1e-06)
            for h in range(2):
                for c in range(chunks):
                    low = (r // 8 + h) * pitch + c * PITCH
                    rows[low : low + 8, :] = scaled[h * 8 : h * 8 + 8, c * LANES : (c + 1) * LANES]
    place.wait()
    batch = 16

    def move(i, _):
        got = [rows[pl.ds((i * (batch // 8) + u // 8) * pitch + u % 8, chunks, stride=PITCH), :] for u in range(batch)]
        for u in range(batch):
            slots[pl.ds(where[0, i * batch + u], chunks, stride=PITCH), :] = got[u]
        return 0

    lax.fori_loop(0, n // batch, move, 0, unroll=n // batch)

    out_parts = out_sem.shape[0]
    out_step = total // out_parts
    stores = []
    for p in range(out_parts):

        def pack(i, _):
            r = pl.multiple_of(p * out_step + i * 16, 16)
            base = (r >> 3) * pitch
            low = [slots[pl.ds(base + c * PITCH, 8), :] for c in range(chunks)]
            high = [slots[pl.ds(base + pitch + c * PITCH, 8), :] for c in range(chunks)]
            both = [jnp.concatenate([a, b], axis=0).astype(jnp.bfloat16) for a, b in zip(low, high)]
            for c in range(chunks):
                obuf[pl.ds(r, 16), c * LANES : (c + 1) * LANES] = both[c]
            return 0

        lax.fori_loop(0, out_step // 16, pack, 0, unroll=out_step // 16)
        store = pltpu.make_async_copy(
            obuf.at[pl.ds(p * out_step, out_step)], out_hbm.at[pl.ds(p * out_step, out_step)], out_sem.at[p]
        )
        store.start()
        stores.append(store)
    for store in stores:
        store.wait()


def prep(x, labels, clusters):
    n, width = x.shape
    total = clusters * MOST
    chunks = width // LANES
    return pl.pallas_call(
        prep_kernel,
        out_shape=(
            jax.ShapeDtypeStruct((total, width), jnp.bfloat16),
            jax.ShapeDtypeStruct((1, n), jnp.int32),
        ),
        in_specs=[pl.BlockSpec(memory_space=pl.ANY), pl.BlockSpec(memory_space=pltpu.HBM)],
        out_specs=(pl.BlockSpec(memory_space=pl.ANY), pl.BlockSpec(memory_space=pltpu.VMEM)),
        scratch_shapes=[
            pltpu.VMEM((n, width), jnp.bfloat16),
            pltpu.VMEM((1, n), jnp.int32),
            pltpu.VMEM((1, n), jnp.int32),
            pltpu.VMEM((n * PITCH // 8 * chunks, LANES), jnp.float32),
            pltpu.VMEM((total * PITCH // 8 * chunks, LANES), jnp.float32),
            pltpu.VMEM((total, width), jnp.bfloat16),
            pltpu.SMEM((1, n), jnp.int32),
            pltpu.SemaphoreType.DMA((4,)),
            pltpu.SemaphoreType.DMA((8,)),
            pltpu.SemaphoreType.DMA((2,)),
        ],
        compiler_params=pltpu.CompilerParams(vmem_limit_bytes=60 * 1024 * 1024),
        name="prep",
    )(x, labels)


def near_kernel(x_ref, out_ref, bias, row_best, col_best, packed):
    sources, pair, width = x_ref.shape
    per = pair // MOST
    tile = 256
    from_each = tile // MOST
    blocks = sources // from_each
    contract = (((1,), (1,)), ((), ()))
    first = (lax.broadcasted_iota(jnp.int32, (8, LANES), 1) == 0).astype(jnp.bfloat16)
    diagonal = lax.broadcasted_iota(jnp.int32, (tile, tile), 0) == lax.broadcasted_iota(jnp.int32, (tile, tile), 1)

    def members(k, b):
        return x_ref[b * from_each : (b + 1) * from_each, k * MOST : (k + 1) * MOST, :].reshape(tile, width)

    for k in range(per):
        for b in range(blocks):
            mine = members(k, b)
            row_mark = mine[:, 0:1].astype(jnp.float32)
            bias[k, b * tile : (b + 1) * tile, :] = jnp.broadcast_to(jnp.where(row_mark > 1.5, FAR, 0.0), (tile, LANES))
            col_mark = lax.dot_general(first, mine[:, :LANES], contract, preferred_element_type=jnp.float32)[0:1]
            col_bias = jnp.where(col_mark > 1.5, FAR, 0.0)
            best = jnp.full((8, tile), -1.0, jnp.float32)
            for a in [b] + list(range(b)):
                similar = lax.dot_general(members(k, a), mine, contract, preferred_element_type=jnp.float32)
                if a == b:
                    similar = jnp.where(diagonal, FAR, similar)
                across = similar + col_bias
                across = jnp.maximum(across[:, :LANES], across[:, LANES:])
                if a == b:
                    row_best[k, a * tile : (a + 1) * tile, :] = across
                else:
                    row_best[k, a * tile : (a + 1) * tile, :] = jnp.maximum(
                        row_best[k, a * tile : (a + 1) * tile, :], across
                    )
                    down = similar + bias[k, a * tile : (a + 1) * tile, 0:1]
                    best = jnp.maximum(best, jnp.max(down.reshape(tile // 8, 8, tile), axis=0))
            col_best[k : k + 1, b * tile : (b + 1) * tile] = jnp.max(best, axis=0, keepdims=True)
        for b in range(blocks):
            across = jnp.max(row_best[k, b * tile : (b + 1) * tile, :].T, axis=0, keepdims=True)
            best = jnp.maximum(across, col_best[k : k + 1, b * tile : (b + 1) * tile])
            for h in range(tile // LANES):
                q = b * (tile // LANES) + h
                packed[k, q : q + 1, :] = best[:, h * LANES : (h + 1) * LANES]
        for g in range(LANES // MOST):
            out_ref[:, g, k * MOST : (k + 1) * MOST] = packed[k, :, g * MOST : (g + 1) * MOST]


def near(x, per):
    sources, pair, width = x.shape
    n = sources * MOST
    group = LANES // MOST
    return pl.pallas_call(
        near_kernel,
        out_shape=jax.ShapeDtypeStruct((sources // group, group, pair), jnp.float32),
        in_specs=[pl.BlockSpec(memory_space=pltpu.VMEM)],
        out_specs=pl.BlockSpec(memory_space=pltpu.VMEM),
        scratch_shapes=[
            pltpu.VMEM((per, n, LANES), jnp.float32),
            pltpu.VMEM((per, n, LANES), jnp.float32),
            pltpu.VMEM((per, n), jnp.float32),
            pltpu.VMEM((per, n // LANES, LANES), jnp.float32),
        ],
        compiler_params=pltpu.CompilerParams(vmem_limit_bytes=16 * 1024 * 1024),
        name="near",
    )(x)


def pick_kernel(x_ref, target_ref, out_ref):
    owners, pair = x_ref.shape
    n = target_ref.shape[1]
    table = x_ref[...].T
    hi = table.astype(jnp.bfloat16)
    rest = table - hi.astype(jnp.float32)
    mid = rest.astype(jnp.bfloat16)
    low = (rest - mid.astype(jnp.float32)).astype(jnp.bfloat16)
    split = jnp.concatenate([hi, mid, low], axis=0)
    shift = pair.bit_length() - 1
    span = 1024
    owner = lax.broadcasted_iota(jnp.int32, (owners, span), 0)
    slot = lax.broadcasted_iota(jnp.int32, (pair, span), 0)
    for b in range(n // span):
        target = target_ref[:, b * span : (b + 1) * span]
        hot = jnp.where(owner == target >> shift, 1.0, 0.0).astype(jnp.bfloat16)
        got = jnp.dot(split, hot, preferred_element_type=jnp.float32)
        value = (got[:pair] + got[pair : 2 * pair]) + got[2 * pair :]
        out_ref[:, b * span : (b + 1) * span] = jnp.sum(
            jnp.where(slot == (target & (pair - 1)), value, 0.0), axis=0, keepdims=True
        )


def pick(x, target):
    return pl.pallas_call(
        pick_kernel,
        out_shape=jax.ShapeDtypeStruct(target.shape, jnp.float32),
        name="pick",
    )(x, target)


def per_device(embeddings, cluster_ids):
    n = embeddings.shape[0]
    axes = ("group", "blk")
    devices = lax.axis_size("group") * lax.axis_size("blk")
    per = CLUSTERS // devices
    outgoing, target = prep(embeddings, cluster_ids.reshape(1, n), CLUSTERS)
    outgoing = outgoing.reshape(devices, per * MOST, -1)
    members = lax.all_to_all(outgoing, axes, split_axis=0, concat_axis=0, tiled=True)
    best = near(members, per).reshape(devices, per * MOST)
    results = lax.all_to_all(best, axes, split_axis=0, concat_axis=0, tiled=True)
    return pick(results, target).reshape(n)


def solution(mesh):
    placed = (P(("group", "blk"), None), P(("group", "blk"), None))
    return jax.shard_map(
        per_device, mesh=mesh, in_specs=placed, out_specs=P(("group", "blk")), check_vma=False
    )
```

```python
import jax
import jax.numpy as jnp
from jax import lax
from jax.experimental import pallas as pl
from jax.experimental.pallas import tpu as pltpu
from jax.sharding import PartitionSpec as P

CLUSTERS = 256
MOST = 16
LANES = 128
PAD = 2.0
FAR = -1000.0
PITCH = 9


def prep_kernel(
    x_hbm, label_hbm, out_ref, target_ref, xbuf, label, at, rows, slots, where, in_sem, small_sem
):
    n, width = x_hbm.shape
    chunks = width // LANES
    total = out_ref.shape[0]
    clusters = total // MOST
    pitch = PITCH * chunks
    parts = in_sem.shape[0]
    step = n // parts
    fetch = pltpu.make_async_copy(label_hbm, label, small_sem.at[0])
    fetch.start()
    loads = [
        pltpu.make_async_copy(x_hbm.at[pl.ds(p * step, step)], xbuf.at[pl.ds(p * step, step)], in_sem.at[p])
        for p in range(parts)
    ]
    for load in loads:
        load.start()

    def fill(i, _):
        base = pl.multiple_of(i * 8 * pitch, 8 * pitch)
        slots[pl.ds(base, 8 * pitch), :] = jnp.full((8 * pitch, LANES), PAD, jnp.float32)
        return 0

    lax.fori_loop(0, total // 64, fill, 0)
    fetch.wait()
    span = 256
    before = (
        lax.broadcasted_iota(jnp.int32, (span, span), 0) < lax.broadcasted_iota(jnp.int32, (span, span), 1)
    ).astype(jnp.bfloat16)
    carry = jnp.zeros((clusters, 1), jnp.float32)
    cluster = lax.broadcasted_iota(jnp.int32, (clusters, span), 0)
    for b in range(n // span):
        name = label[:, b * span : (b + 1) * span]
        hit = cluster == name
        hot = jnp.where(hit, 1.0, 0.0)
        count = jnp.dot(hot.astype(jnp.bfloat16), before, preferred_element_type=jnp.float32) + carry
        rank = jnp.sum(jnp.where(hit, count, 0.0), axis=0, keepdims=True)
        carry = carry + jnp.sum(hot, axis=1, keepdims=True)
        target = name * MOST + rank.astype(jnp.int32)
        target_ref[:, b * span : (b + 1) * span] = target
        at[:, b * span : (b + 1) * span] = (target >> 3) * pitch + (target & 7)
    place = pltpu.make_async_copy(at, where, small_sem.at[1])
    place.start()

    for p in range(parts):
        loads[p].wait()

        for r in range(p * step, (p + 1) * step, 16):
            wide = xbuf[r : r + 16, :].astype(jnp.float32)
            scaled = wide * lax.rsqrt(jnp.sum(wide * wide, axis=1, keepdims=True) + 1e-06)
            for h in range(2):
                for c in range(chunks):
                    low = (r // 8 + h) * pitch + c * PITCH
                    rows[low : low + 8, :] = scaled[h * 8 : h * 8 + 8, c * LANES : (c + 1) * LANES]
    place.wait()
    batch = 16

    def move(i, _):
        got = [rows[pl.ds((i * (batch // 8) + u // 8) * pitch + u % 8, chunks, stride=PITCH), :] for u in range(batch)]
        for u in range(batch):
            slots[pl.ds(where[0, i * batch + u], chunks, stride=PITCH), :] = got[u]
        return 0

    lax.fori_loop(0, n // batch, move, 0, unroll=n // batch)

    for r in range(0, total, 16):
        base = r // 8 * pitch
        low = [slots[base + c * PITCH : base + c * PITCH + 8, :] for c in range(chunks)]
        high = [slots[base + pitch + c * PITCH : base + pitch + c * PITCH + 8, :] for c in range(chunks)]
        both = [jnp.concatenate([a, b], axis=0).astype(jnp.bfloat16) for a, b in zip(low, high)]
        for c in range(chunks):
            out_ref[r : r + 16, c * LANES : (c + 1) * LANES] = both[c]


def prep(x, labels, clusters):
    n, width = x.shape
    total = clusters * MOST
    chunks = width // LANES
    return pl.pallas_call(
        prep_kernel,
        out_shape=(
            jax.ShapeDtypeStruct((total, width), jnp.bfloat16),
            jax.ShapeDtypeStruct((1, n), jnp.int32),
        ),
        in_specs=[pl.BlockSpec(memory_space=pl.ANY), pl.BlockSpec(memory_space=pltpu.HBM)],
        out_specs=(pl.BlockSpec(memory_space=pltpu.VMEM), pl.BlockSpec(memory_space=pltpu.VMEM)),
        scratch_shapes=[
            pltpu.VMEM((n, width), jnp.bfloat16),
            pltpu.VMEM((1, n), jnp.int32),
            pltpu.VMEM((1, n), jnp.int32),
            pltpu.VMEM((n * PITCH // 8 * chunks, LANES), jnp.float32),
            pltpu.VMEM((total * PITCH // 8 * chunks, LANES), jnp.float32),
            pltpu.SMEM((1, n), jnp.int32),
            pltpu.SemaphoreType.DMA((4,)),
            pltpu.SemaphoreType.DMA((2,)),
        ],
        compiler_params=pltpu.CompilerParams(vmem_limit_bytes=44 * 1024 * 1024),
        name="prep",
    )(x, labels)


def near_kernel(x_ref, out_ref, bias, row_best, col_best, packed):
    sources, pair, width = x_ref.shape
    per = pair // MOST
    tile = 256
    from_each = tile // MOST
    blocks = sources // from_each
    contract = (((1,), (1,)), ((), ()))
    first = (lax.broadcasted_iota(jnp.int32, (8, LANES), 1) == 0).astype(jnp.bfloat16)
    diagonal = lax.broadcasted_iota(jnp.int32, (tile, tile), 0) == lax.broadcasted_iota(jnp.int32, (tile, tile), 1)

    def members(k, b):
        return x_ref[b * from_each : (b + 1) * from_each, k * MOST : (k + 1) * MOST, :].reshape(tile, width)

    for k in range(per):
        for b in range(blocks):
            mine = members(k, b)
            row_mark = mine[:, 0:1].astype(jnp.float32)
            bias[k, b * tile : (b + 1) * tile, :] = jnp.broadcast_to(jnp.where(row_mark > 1.5, FAR, 0.0), (tile, LANES))
            col_mark = lax.dot_general(first, mine[:, :LANES], contract, preferred_element_type=jnp.float32)[0:1]
            col_bias = jnp.where(col_mark > 1.5, FAR, 0.0)
            best = jnp.full((8, tile), -1.0, jnp.float32)
            for a in [b] + list(range(b)):
                similar = lax.dot_general(members(k, a), mine, contract, preferred_element_type=jnp.float32)
                if a == b:
                    similar = jnp.where(diagonal, FAR, similar)
                across = similar + col_bias
                across = jnp.maximum(across[:, :LANES], across[:, LANES:])
                if a == b:
                    row_best[k, a * tile : (a + 1) * tile, :] = across
                else:
                    row_best[k, a * tile : (a + 1) * tile, :] = jnp.maximum(
                        row_best[k, a * tile : (a + 1) * tile, :], across
                    )
                    down = similar + bias[k, a * tile : (a + 1) * tile, 0:1]
                    best = jnp.maximum(best, jnp.max(down.reshape(tile // 8, 8, tile), axis=0))
            col_best[k : k + 1, b * tile : (b + 1) * tile] = jnp.max(best, axis=0, keepdims=True)
        for b in range(blocks):
            across = jnp.max(row_best[k, b * tile : (b + 1) * tile, :].T, axis=0, keepdims=True)
            best = jnp.maximum(across, col_best[k : k + 1, b * tile : (b + 1) * tile])
            for h in range(tile // LANES):
                q = b * (tile // LANES) + h
                packed[k, q : q + 1, :] = best[:, h * LANES : (h + 1) * LANES]
        for g in range(LANES // MOST):
            out_ref[:, g, k * MOST : (k + 1) * MOST] = packed[k, :, g * MOST : (g + 1) * MOST]


def near(x, per):
    sources, pair, width = x.shape
    n = sources * MOST
    group = LANES // MOST
    return pl.pallas_call(
        near_kernel,
        out_shape=jax.ShapeDtypeStruct((sources // group, group, pair), jnp.float32),
        in_specs=[pl.BlockSpec(memory_space=pltpu.VMEM)],
        out_specs=pl.BlockSpec(memory_space=pltpu.VMEM),
        scratch_shapes=[
            pltpu.VMEM((per, n, LANES), jnp.float32),
            pltpu.VMEM((per, n, LANES), jnp.float32),
            pltpu.VMEM((per, n), jnp.float32),
            pltpu.VMEM((per, n // LANES, LANES), jnp.float32),
        ],
        compiler_params=pltpu.CompilerParams(vmem_limit_bytes=16 * 1024 * 1024),
        name="near",
    )(x)


def pick_kernel(x_ref, target_ref, out_ref):
    owners, pair = x_ref.shape
    n = target_ref.shape[1]
    table = x_ref[...].T
    hi = table.astype(jnp.bfloat16)
    rest = table - hi.astype(jnp.float32)
    mid = rest.astype(jnp.bfloat16)
    low = (rest - mid.astype(jnp.float32)).astype(jnp.bfloat16)
    split = jnp.concatenate([hi, mid, low], axis=0)
    shift = pair.bit_length() - 1
    span = 1024
    owner = lax.broadcasted_iota(jnp.int32, (owners, span), 0)
    slot = lax.broadcasted_iota(jnp.int32, (pair, span), 0)
    for b in range(n // span):
        target = target_ref[:, b * span : (b + 1) * span]
        hot = jnp.where(owner == target >> shift, 1.0, 0.0).astype(jnp.bfloat16)
        got = jnp.dot(split, hot, preferred_element_type=jnp.float32)
        value = (got[:pair] + got[pair : 2 * pair]) + got[2 * pair :]
        out_ref[:, b * span : (b + 1) * span] = jnp.sum(
            jnp.where(slot == (target & (pair - 1)), value, 0.0), axis=0, keepdims=True
        )


def pick(x, target):
    return pl.pallas_call(
        pick_kernel,
        out_shape=jax.ShapeDtypeStruct(target.shape, jnp.float32),
        name="pick",
    )(x, target)


def per_device(embeddings, cluster_ids):
    n = embeddings.shape[0]
    axes = ("group", "blk")
    devices = lax.axis_size("group") * lax.axis_size("blk")
    per = CLUSTERS // devices
    rows = pltpu.with_memory_space_constraint(embeddings, pltpu.HBM)
    labels = pltpu.with_memory_space_constraint(cluster_ids.reshape(1, n), pltpu.HBM)
    outgoing, target = prep(rows, labels, CLUSTERS)
    outgoing = outgoing.reshape(devices, per * MOST, -1)
    members = lax.all_to_all(outgoing, axes, split_axis=0, concat_axis=0, tiled=True)
    best = near(members, per).reshape(devices, per * MOST)
    results = lax.all_to_all(best, axes, split_axis=0, concat_axis=0, tiled=True)
    return pick(results, target).reshape(n)


def solution(mesh):
    placed = (P(("group", "blk"), None), P(("group", "blk"), None))
    return jax.shard_map(
        per_device, mesh=mesh, in_specs=placed, out_specs=P(("group", "blk")), check_vma=False
    )
```

```python
import jax
import jax.numpy as jnp
from jax import lax
from jax.experimental import pallas as pl
from jax.experimental.pallas import tpu as pltpu
from jax.sharding import PartitionSpec as P

CLUSTERS = 256
MOST = 16
LANES = 128
PAD = 2.0
FAR = -1000.0
PITCH = 9


def prep_kernel(
    x_hbm, label_hbm, out_ref, target_ref, xbuf, label, at, rows, slots, where, in_sem, small_sem
):
    n, width = x_hbm.shape
    chunks = width // LANES
    total = out_ref.shape[0]
    clusters = total // MOST
    pitch = PITCH * chunks
    parts = in_sem.shape[0]
    step = n // parts
    fetch = pltpu.make_async_copy(label_hbm, label, small_sem.at[0])
    fetch.start()
    loads = [
        pltpu.make_async_copy(x_hbm.at[pl.ds(p * step, step)], xbuf.at[pl.ds(p * step, step)], in_sem.at[p])
        for p in range(parts)
    ]
    for load in loads:
        load.start()

    def fill(i, _):
        base = pl.multiple_of(i * 8 * pitch, 8 * pitch)
        slots[pl.ds(base, 8 * pitch), :] = jnp.full((8 * pitch, LANES), PAD, jnp.float32)
        return 0

    lax.fori_loop(0, total // 64, fill, 0)
    fetch.wait()
    span = 256
    before = (
        lax.broadcasted_iota(jnp.int32, (span, span), 0) < lax.broadcasted_iota(jnp.int32, (span, span), 1)
    ).astype(jnp.bfloat16)
    carry = jnp.zeros((clusters, 1), jnp.float32)
    cluster = lax.broadcasted_iota(jnp.int32, (clusters, span), 0)
    for b in range(n // span):
        name = label[:, b * span : (b + 1) * span]
        hit = cluster == name
        hot = jnp.where(hit, 1.0, 0.0)
        count = jnp.dot(hot.astype(jnp.bfloat16), before, preferred_element_type=jnp.float32) + carry
        rank = jnp.sum(jnp.where(hit, count, 0.0), axis=0, keepdims=True)
        carry = carry + jnp.sum(hot, axis=1, keepdims=True)
        target = name * MOST + rank.astype(jnp.int32)
        target_ref[:, b * span : (b + 1) * span] = target
        at[:, b * span : (b + 1) * span] = (target >> 3) * pitch + (target & 7)
    place = pltpu.make_async_copy(at, where, small_sem.at[1])
    place.start()

    for p in range(parts):
        loads[p].wait()

        for r in range(p * step, (p + 1) * step, 16):
            wide = xbuf[r : r + 16, :].astype(jnp.float32)
            scaled = wide * lax.rsqrt(jnp.sum(wide * wide, axis=1, keepdims=True) + 1e-06)
            for h in range(2):
                for c in range(chunks):
                    low = (r // 8 + h) * pitch + c * PITCH
                    rows[low : low + 8, :] = scaled[h * 8 : h * 8 + 8, c * LANES : (c + 1) * LANES]
    place.wait()
    batch = 16

    def move(i, _):
        got = [rows[pl.ds((i * (batch // 8) + u // 8) * pitch + u % 8, chunks, stride=PITCH), :] for u in range(batch)]
        for u in range(batch):
            slots[pl.ds(where[0, i * batch + u], chunks, stride=PITCH), :] = got[u]
        return 0

    lax.fori_loop(0, n // batch, move, 0, unroll=n // batch)

    for r in range(0, total, 16):
        base = r // 8 * pitch
        low = [slots[base + c * PITCH : base + c * PITCH + 8, :] for c in range(chunks)]
        high = [slots[base + pitch + c * PITCH : base + pitch + c * PITCH + 8, :] for c in range(chunks)]
        both = [jnp.concatenate([a, b], axis=0).astype(jnp.bfloat16) for a, b in zip(low, high)]
        for c in range(chunks):
            out_ref[r : r + 16, c * LANES : (c + 1) * LANES] = both[c]


def prep(x, labels, clusters):
    n, width = x.shape
    total = clusters * MOST
    chunks = width // LANES
    return pl.pallas_call(
        prep_kernel,
        out_shape=(
            jax.ShapeDtypeStruct((total, width), jnp.bfloat16),
            jax.ShapeDtypeStruct((1, n), jnp.int32),
        ),
        in_specs=[pl.BlockSpec(memory_space=pl.ANY), pl.BlockSpec(memory_space=pltpu.HBM)],
        out_specs=(pl.BlockSpec(memory_space=pltpu.VMEM), pl.BlockSpec(memory_space=pltpu.VMEM)),
        scratch_shapes=[
            pltpu.VMEM((n, width), jnp.bfloat16),
            pltpu.VMEM((1, n), jnp.int32),
            pltpu.VMEM((1, n), jnp.int32),
            pltpu.VMEM(((n // 8 + 1) * PITCH * chunks, LANES), jnp.float32),
            pltpu.VMEM(((total // 8 + 1) * PITCH * chunks, LANES), jnp.float32),
            pltpu.SMEM((1, n), jnp.int32),
            pltpu.SemaphoreType.DMA((4,)),
            pltpu.SemaphoreType.DMA((2,)),
        ],
        compiler_params=pltpu.CompilerParams(vmem_limit_bytes=44 * 1024 * 1024),
        name="prep",
    )(x, labels)


def near_kernel(x_ref, out_ref, bias, row_best, col_best, packed):
    sources, pair, width = x_ref.shape
    per = pair // MOST
    tile = 256
    from_each = tile // MOST
    blocks = sources // from_each
    contract = (((1,), (1,)), ((), ()))
    first = (lax.broadcasted_iota(jnp.int32, (8, LANES), 1) == 0).astype(jnp.bfloat16)
    diagonal = lax.broadcasted_iota(jnp.int32, (tile, tile), 0) == lax.broadcasted_iota(jnp.int32, (tile, tile), 1)

    def members(k, b):
        return x_ref[b * from_each : (b + 1) * from_each, k * MOST : (k + 1) * MOST, :].reshape(tile, width)

    for k in range(per):
        for b in range(blocks):
            mine = members(k, b)
            row_mark = mine[:, 0:1].astype(jnp.float32)
            bias[k, b * tile : (b + 1) * tile, :] = jnp.broadcast_to(jnp.where(row_mark > 1.5, FAR, 0.0), (tile, LANES))
            col_mark = lax.dot_general(first, mine[:, :LANES], contract, preferred_element_type=jnp.float32)[0:1]
            col_bias = jnp.where(col_mark > 1.5, FAR, 0.0)
            best = jnp.full((8, tile), -1.0, jnp.float32)
            for a in [b] + list(range(b)):
                similar = lax.dot_general(members(k, a), mine, contract, preferred_element_type=jnp.float32)
                if a == b:
                    similar = jnp.where(diagonal, FAR, similar)
                across = similar + col_bias
                across = jnp.maximum(across[:, :LANES], across[:, LANES:])
                if a == b:
                    row_best[k, a * tile : (a + 1) * tile, :] = across
                else:
                    row_best[k, a * tile : (a + 1) * tile, :] = jnp.maximum(
                        row_best[k, a * tile : (a + 1) * tile, :], across
                    )
                    down = similar + bias[k, a * tile : (a + 1) * tile, 0:1]
                    best = jnp.maximum(best, jnp.max(down.reshape(tile // 8, 8, tile), axis=0))
            col_best[k : k + 1, b * tile : (b + 1) * tile] = jnp.max(best, axis=0, keepdims=True)
        for b in range(blocks):
            across = jnp.max(row_best[k, b * tile : (b + 1) * tile, :].T, axis=0, keepdims=True)
            best = jnp.maximum(across, col_best[k : k + 1, b * tile : (b + 1) * tile])
            for h in range(tile // LANES):
                q = b * (tile // LANES) + h
                packed[k, q : q + 1, :] = best[:, h * LANES : (h + 1) * LANES]
        for g in range(LANES // MOST):
            out_ref[:, g, k * MOST : (k + 1) * MOST] = packed[k, :, g * MOST : (g + 1) * MOST]


def near(x, per):
    sources, pair, width = x.shape
    n = sources * MOST
    group = LANES // MOST
    return pl.pallas_call(
        near_kernel,
        out_shape=jax.ShapeDtypeStruct((sources // group, group, pair), jnp.float32),
        in_specs=[pl.BlockSpec(memory_space=pltpu.VMEM)],
        out_specs=pl.BlockSpec(memory_space=pltpu.VMEM),
        scratch_shapes=[
            pltpu.VMEM((per, n, LANES), jnp.float32),
            pltpu.VMEM((per, n, LANES), jnp.float32),
            pltpu.VMEM((per, n), jnp.float32),
            pltpu.VMEM((per, n // LANES, LANES), jnp.float32),
        ],
        compiler_params=pltpu.CompilerParams(vmem_limit_bytes=16 * 1024 * 1024),
        name="near",
    )(x)


def pick_kernel(x_ref, target_ref, out_ref):
    owners, pair = x_ref.shape
    n = target_ref.shape[1]
    table = x_ref[...].T
    hi = table.astype(jnp.bfloat16)
    rest = table - hi.astype(jnp.float32)
    mid = rest.astype(jnp.bfloat16)
    low = (rest - mid.astype(jnp.float32)).astype(jnp.bfloat16)
    split = jnp.concatenate([hi, mid, low], axis=0)
    shift = pair.bit_length() - 1
    span = 1024
    owner = lax.broadcasted_iota(jnp.int32, (owners, span), 0)
    slot = lax.broadcasted_iota(jnp.int32, (pair, span), 0)
    for b in range(n // span):
        target = target_ref[:, b * span : (b + 1) * span]
        hot = jnp.where(owner == target >> shift, 1.0, 0.0).astype(jnp.bfloat16)
        got = jnp.dot(split, hot, preferred_element_type=jnp.float32)
        value = (got[:pair] + got[pair : 2 * pair]) + got[2 * pair :]
        out_ref[:, b * span : (b + 1) * span] = jnp.sum(
            jnp.where(slot == (target & (pair - 1)), value, 0.0), axis=0, keepdims=True
        )


def pick(x, target):
    return pl.pallas_call(
        pick_kernel,
        out_shape=jax.ShapeDtypeStruct(target.shape, jnp.float32),
        name="pick",
    )(x, target)


def per_device(embeddings, cluster_ids):
    n = embeddings.shape[0]
    axes = ("group", "blk")
    devices = lax.axis_size("group") * lax.axis_size("blk")
    per = CLUSTERS // devices
    rows = pltpu.with_memory_space_constraint(embeddings, pltpu.HBM)
    labels = pltpu.with_memory_space_constraint(cluster_ids.reshape(1, n), pltpu.HBM)
    outgoing, target = prep(rows, labels, CLUSTERS)
    outgoing = outgoing.reshape(devices, per * MOST, -1)
    members = lax.all_to_all(outgoing, axes, split_axis=0, concat_axis=0, tiled=True)
    best = near(members, per).reshape(devices, per * MOST)
    results = lax.all_to_all(best, axes, split_axis=0, concat_axis=0, tiled=True)
    return pick(results, target).reshape(n)


def solution(mesh):
    placed = (P(("group", "blk"), None), P(("group", "blk"), None))
    return jax.shard_map(
        per_device, mesh=mesh, in_specs=placed, out_specs=P(("group", "blk")), check_vma=False
    )
```
